32 devices in a mesh: groups: 2 (over y), dp: 4 (over z), tensor: 4 (over x, core).
Axes of the slice: x: 2, y: 2, z: 4, core: 2. Of those that a mesh axis runs over, the one named last changes fastest.
Arguments:
- query: bfloat16 [4, 32, 64, 128], P(None, ('groups', 'dp'), 'tensor'), parts along dimension 1, may hold values from -72 to 72
- new_kv: bfloat16 [4, 32, 8, 256], P(None, ('groups', 'dp'), 'tensor'), parts along dimension 1, may hold values from -18 to 18
- tail_pool: bfloat16 [64, 4, 8, 256], P(('groups', 'dp'), None, 'tensor'), parts along dimension 0, may hold values from -18 to 18
- page_table: int32 [32, 2], P(('groups', 'dp')), parts along dimension 0, may hold values from 0 to 7, as said below
- tail_len: int32 [32], P(('groups', 'dp')), parts along dimension 0, may hold values from 1 to 4, as said below
- fork_parent: int32 [4, 32], P(None, 'groups'), parts along dimension 1, may hold values from -1 to 15, as said below
- prompt_kv: bfloat16 [4096, 8, 256], P('groups', 'tensor'), parts along dimension 0, may hold values from -6 to 6
- out_weight: bfloat16 [8192, 8192], P('tensor', 'dp'), may hold values from -0.0625 to 0.0625
- residual: bfloat16 [4, 32, 8192], P(None, ('groups', 'tensor'), 'dp'), parts along dimension 1, may hold values from -1.5 to 1.5
Outputs:
- mixed: bfloat16 [4, 32, 8192], P(None, ('groups', 'tensor'), 'dp'), parts along dimension 1
The draws below stay inside these ranges and needn't reach their ends.
There are 2 independent parts, one for each index of `groups`. The reference program is written for one: setup_inputs(seed, part) draws one part's arguments, and reference() takes and returns one part's arrays. A program takes and returns all parts, laid end to end along the dimension named above; an argument that names none is the same for every part. Nothing has to cross between parts.
Inputs may be any that keep to these rules, and one draw needn't show every extreme that they name: `page_table`: for each node's owner, the rows of the nodes of one index of dp form a permutation of 0 to 7. `tail_len`: some node has exactly 4 tokens. `fork_parent`: at each step every index of dp holds exactly one node with a value other than -1, and all values that name nodes of one index of dp at one step name the same node.
All inputs are finite; a program needn't handle non-finite values.
Results may differ from the reference program's by a relative error of at most 0.013.
Values may be sent and summed in bfloat16 or wider, within the bound.
A program may use at most 64 MiB of HBM per device.

```python
import math
import jax
import jax.numpy as jnp
from jax import lax

D = 8192
HEADS = 64
KV_HEADS = 8
HEAD_DIM = 128
NODES_DEV = 4
PROMPT = 2048
STEPS = 4
PAGE = 4
TAIL_PAGES = 2
NODES = 16


anchor_total = 8


def anchor_signs(key):
    bits = jax.random.randint(key, (anchor_total, KV_HEADS, HEAD_DIM), 0, 2)
    return (2 * bits - 1).astype(jnp.float32)


def anchor_levels(lowest, spacing):
    return lowest + spacing * (jnp.arange(anchor_total) % 4).astype(jnp.float32)


def draw_query(key, part):
    signs = anchor_signs(key)
    key = jax.random.fold_in(key, 29)
    base_key, mark_key, pick_key = jax.random.split(key, 3)
    shape = (STEPS, NODES, HEADS, HEAD_DIM)
    base = jnp.clip(jax.random.normal(base_key, shape, jnp.float32), -6.0, 6.0)
    targets = anchor_levels(120.0, 40.0)
    aligned = jax.random.randint(mark_key, (STEPS, NODES, HEADS), 0, 8) == 0
    picked = jax.random.randint(pick_key, (STEPS, NODES, HEADS), 0, anchor_total)
    kv_of_head = jnp.arange(HEADS) // (HEADS // KV_HEADS)
    strength = targets / math.sqrt(HEAD_DIM)
    target_rows = signs[picked, kv_of_head[None, None, :]] * strength[picked][..., None]
    return jnp.where(aligned[..., None], target_rows, base).astype(jnp.bfloat16)


def draw_prompt_kv(key, part):
    signs = anchor_signs(key)
    key = jax.random.fold_in(key, 23)
    base_key, place_key = jax.random.split(key)
    shape = (PROMPT, KV_HEADS, 2 * HEAD_DIM)
    base = jnp.clip(jax.random.normal(base_key, shape, jnp.float32), -6.0, 6.0)
    targets = anchor_levels(120.0, 40.0)
    order = jax.random.permutation(place_key, PROMPT)
    first = order[:anchor_total]
    second = order[anchor_total:2 * anchor_total]
    ratio = 1.0 - 2.0 * HEAD_DIM / targets
    nearby = signs.at[:, :, 0].multiply(ratio[:, None])
    keys = base[..., :HEAD_DIM]
    keys = keys.at[first].set(signs)
    keys = keys.at[second].set(nearby)
    return jnp.concatenate([keys, base[..., HEAD_DIM:]], axis=-1).astype(jnp.bfloat16)


def draw_page_table(key, part):
    key = jax.random.fold_in(key, 17)
    device_count = NODES // NODES_DEV
    device_keys = jax.random.split(key, device_count)
    shuffled = jax.vmap(lambda single: jax.random.permutation(single, NODES_DEV * TAIL_PAGES))(device_keys)
    return shuffled.reshape(NODES, TAIL_PAGES).astype(jnp.int32)


def draw_tail_len(key, part):
    key = jax.random.fold_in(key, 13)
    first_key, second_key = jax.random.split(key)
    longest = TAIL_PAGES * PAGE - STEPS
    lengths = jax.random.randint(first_key, (NODES,), 1, longest + 1)
    chosen = jax.random.randint(second_key, (), 0, NODES)
    lengths = jnp.where(jnp.arange(NODES) == chosen, longest, lengths)
    return lengths.astype(jnp.int32)


def draw_fork_parent(key, part):
    key = jax.random.fold_in(key, 11)
    device_count = NODES // NODES_DEV
    first_key, second_key, third_key = jax.random.split(key, 3)
    device_base = jnp.arange(device_count, dtype=jnp.int32) * NODES_DEV
    expanded = jax.random.randint(first_key, (STEPS, device_count), 0, NODES_DEV) + device_base[None, :]
    children = jax.random.randint(second_key, (STEPS, device_count), 0, NODES_DEV) + device_base[None, :]
    source_device = jax.random.randint(third_key, (STEPS, device_count), 0, device_count)
    child_parent = jnp.take_along_axis(expanded, source_device, axis=1)
    node_ids = jnp.arange(NODES, dtype=jnp.int32)
    owners = node_ids // NODES_DEV
    child_here = children[:, owners]
    parent_here = child_parent[:, owners]
    return jnp.where(node_ids[None, :] == child_here, parent_here, -1).astype(jnp.int32)


def level_of(own_key, dims, shards, least, largest):
    gain, own = 1.0, jax.random.fold_in(own_key, 6)
    for axis_at, parts in shards:
        steps = jnp.exp(jax.random.uniform(jax.random.fold_in(own, axis_at), (parts,), jnp.float32, least / len(shards), largest / len(shards)))
        gain = gain * jnp.repeat(steps, dims[axis_at] // parts).reshape([-1 if axis == axis_at else 1 for axis in range(len(dims))])
    return gain


def scatter_about(stream_key, shape, scale, limit, shards=(), kind=jnp.bfloat16):
    array = scale * jax.random.normal(stream_key, shape, jnp.float32)
    if shards:
        array = array * level_of(stream_key, shape, shards, -0.22, 0.18)
    return jnp.clip(array, -limit, limit).astype(kind)


def setup_inputs(seed: int = 0, part: int = 0) -> dict:
    key_of = jax.random.split(jax.random.key(seed), 10)
    part_keys = jax.random.split(jax.random.fold_in(key_of[9], part), 10)
    query = draw_query(jax.random.fold_in(jax.random.fold_in(key_of[9], part), 71), part)
    new_kv = scatter_about(part_keys[1], (STEPS, NODES, KV_HEADS, 2 * HEAD_DIM), 3.0, 18.0, ((1, 4), (2, 4)))
    tail_pool = scatter_about(part_keys[2], (NODES * TAIL_PAGES, PAGE, KV_HEADS, 2 * HEAD_DIM), 3.0, 18.0, ((0, 4), (2, 4)))
    page_table = draw_page_table(jax.random.fold_in(jax.random.fold_in(key_of[9], part), 71), part)
    tail_len = draw_tail_len(jax.random.fold_in(jax.random.fold_in(key_of[9], part), 71), part)
    fork_parent = draw_fork_parent(jax.random.fold_in(jax.random.fold_in(key_of[9], part), 71), part)
    prompt_kv = draw_prompt_kv(jax.random.fold_in(jax.random.fold_in(key_of[9], part), 71), part)
    out_weight = scatter_about(key_of[7], (HEADS * HEAD_DIM, D), (HEADS * HEAD_DIM) ** -0.5, 0.0625, ((0, 4), (1, 4)))
    residual = scatter_about(part_keys[8], (STEPS, NODES, D), 0.25, 1.5, ((1, 4), (2, 4)))
    return {"query": query, "new_kv": new_kv, "tail_pool": tail_pool, "page_table": page_table, "tail_len": tail_len, "fork_parent": fork_parent, "prompt_kv": prompt_kv, "out_weight": out_weight, "residual": residual}


def attend_nodes(queries, tail_cache, visible, prompt_kv):
    head_dim = queries.shape[-1]
    kv_count = prompt_kv.shape[1]
    node_count = queries.shape[0]
    group_size = queries.shape[1] // kv_count
    score_scale = head_dim ** -0.5
    grouped = queries.reshape(node_count, kv_count, group_size, head_dim).astype(jnp.float32)
    prompt_keys = prompt_kv[..., :head_dim].astype(jnp.float32)
    prompt_values = prompt_kv[..., head_dim:].astype(jnp.float32)
    tail_keys = tail_cache[..., :head_dim].astype(jnp.float32)
    tail_values = tail_cache[..., head_dim:].astype(jnp.float32)
    prompt_scores = jnp.einsum('bkgd,pkd->bkgp', grouped, prompt_keys) * score_scale
    tail_scores = jnp.einsum('bkgd,btkd->bkgt', grouped, tail_keys) * score_scale
    tail_scores = jnp.where(visible[:, None, None, :], tail_scores, -jnp.inf)
    highest = jnp.maximum(prompt_scores.max(-1), tail_scores.max(-1))
    prompt_weights = jnp.exp(prompt_scores - highest[..., None])
    tail_weights = jnp.exp(tail_scores - highest[..., None])
    denominator = prompt_weights.sum(-1) + tail_weights.sum(-1)
    rounded_prompt = lax.optimization_barrier(prompt_weights.astype(jnp.bfloat16)).astype(jnp.float32)
    rounded_tail = lax.optimization_barrier(tail_weights.astype(jnp.bfloat16)).astype(jnp.float32)
    mixed_values = jnp.einsum('bkgp,pkd->bkgd', rounded_prompt, prompt_values)
    mixed_values = mixed_values + jnp.einsum('bkgt,btkd->bkgd', rounded_tail, tail_values)
    return (mixed_values / denominator[..., None]).reshape(node_count, -1).astype(jnp.bfloat16)


def reference(query, new_kv, tail_pool, page_table, tail_len, fork_parent, prompt_kv, out_weight, residual):
    tail_tokens = TAIL_PAGES * PAGE
    node_ids = jnp.arange(NODES, dtype=jnp.int32)
    page_base = (node_ids // NODES_DEV) * (NODES_DEV * TAIL_PAGES)
    physical = (page_table + page_base[:, None]).reshape(-1).astype(jnp.int32)
    tail_cache = tail_pool[physical].reshape(NODES, tail_tokens, KV_HEADS, 2 * HEAD_DIM)
    lengths = tail_len
    positions = jnp.arange(tail_tokens, dtype=jnp.int32)
    blocks = NODES // NODES_DEV

    def one_block(members):
        return attend_nodes(members[0], members[1], members[2], prompt_kv)

    outputs = []
    for moment in range(STEPS):
        parents = fork_parent[moment]
        source = jnp.where(parents >= 0, parents, node_ids)
        tail_cache = tail_cache[source]
        lengths = lengths[source]
        landing = positions[None, :] == lengths[:, None]
        tail_cache = jnp.where(landing[:, :, None, None], new_kv[moment][:, None], tail_cache)
        visible = positions[None, :] <= lengths[:, None]
        attended = lax.map(one_block, (
            query[moment].reshape(blocks, NODES_DEV, HEADS, HEAD_DIM),
            tail_cache.reshape(blocks, NODES_DEV, tail_tokens, KV_HEADS, 2 * HEAD_DIM),
            visible.reshape(blocks, NODES_DEV, tail_tokens)))
        outputs.append(attended.reshape(NODES, HEADS * HEAD_DIM))
        lengths = lengths + 1
    head_outputs = jnp.stack(outputs).reshape(STEPS * NODES, HEADS * HEAD_DIM)
    projected = jnp.dot(head_outputs, out_weight, preferred_element_type=jnp.float32)
    projected = projected.reshape(STEPS, NODES, D)
    return (residual.astype(jnp.float32) + projected).astype(jnp.bfloat16)
```

```python
import functools
import math

import jax
import jax.numpy as jnp
from jax import lax
from jax.experimental import pallas as pl
from jax.experimental.pallas import tpu as pltpu
from jax.sharding import PartitionSpec as P

MESH = pl.DeviceIdType.MESH
BLOCK = 128


def kernel(
    dims, q_ref, keys_ref, values_ref, pack_ref, fork_ref, weight_ref, residual_ref, out_ref,
    q_flat, scores, tail_scores, packs, weight, heads, partial, landed,
    weight_sem, own_sem, pack_send, pack_recv, head_send, head_recv, part_send, part_recv,
):
    dp, tensor, steps, nodes, head_count, kv_local, head_dim, pages, page, tile = dims
    pairs = steps * nodes
    rows = pairs * head_count
    group = head_count // kv_local
    pool_rows = pages * page * kv_local
    new_rows = pairs * kv_local
    me = lax.axis_index("dp")
    me_tensor = lax.axis_index("tensor")
    factor = head_dim ** (-0.5) * math.log2(math.e)

    weight_copy = pltpu.make_async_copy(weight_ref, weight, weight_sem)
    weight_copy.start()
    own_copy = pltpu.make_async_copy(pack_ref, packs.at[me], own_sem)
    own_copy.start()

    barrier = pltpu.get_barrier_semaphore()
    for hop in range(1, dp):
        pl.semaphore_signal(
            barrier, inc=1, device_id={"dp": lax.rem(me + hop, dp)}, device_id_type=MESH
        )
    for hop in range(1, tensor):
        pl.semaphore_signal(
            barrier, inc=1, device_id={"tensor": lax.rem(me_tensor + hop, tensor)},
            device_id_type=MESH,
        )
    pl.semaphore_wait(barrier, dp + tensor - 2)

    pack_copies = []
    for hop in range(1, dp):
        copy = pltpu.make_async_remote_copy(
            src_ref=pack_ref,
            dst_ref=packs.at[me],
            send_sem=pack_send.at[hop],
            recv_sem=pack_recv.at[hop],
            device_id={"dp": lax.rem(me + hop, dp)},
            device_id_type=MESH,
        )
        copy.start()
        pack_copies.append(copy)

    q_flat[...] = q_ref[...].astype(jnp.float32)
    q = jnp.concatenate(
        [q_flat[pl.ds(h, pairs, stride=head_count), :] for h in range(head_count)], axis=0
    ).astype(jnp.bfloat16)
    contract = (((1,), (1,)), ((), ()))

    width = scores.shape[2]
    chunks = scores.shape[0]
    row_kv = lax.broadcasted_iota(jnp.int32, (rows, width), 0) // (group * pairs)
    col_kv = lax.broadcasted_iota(jnp.int32, (rows, width), 1) % kv_local
    same = row_kv == col_kv

    def score_chunk(c, highest):
        start = pl.multiple_of(c * width, width)
        s = lax.dot_general(
            q, keys_ref[pl.ds(start, width), :], contract, preferred_element_type=jnp.float32
        )
        s = jnp.where(same, s, -jnp.inf)
        scores[c] = s
        return jnp.maximum(highest, s.max(-1, keepdims=True))

    prompt_max = lax.fori_loop(
        0, chunks, score_chunk, jnp.full((rows, 1), -jnp.inf, jnp.float32)
    )

    def weigh_chunk(c, carry):
        total, acc = carry
        start = pl.multiple_of(c * width, width)
        w = jnp.exp2((scores[c] - prompt_max) * factor)
        total = total + w.sum(-1, keepdims=True)
        acc = acc + jnp.dot(
            w.astype(jnp.bfloat16), values_ref[pl.ds(start, width), :],
            preferred_element_type=jnp.float32,
        )
        return total, acc

    prompt_sum, prompt_acc = lax.fori_loop(
        0, chunks, weigh_chunk,
        (jnp.zeros((rows, 1), jnp.float32), jnp.zeros((rows, head_dim), jnp.float32)),
    )

    forks = fork_ref[...].astype(jnp.float32)
    total_nodes = forks.shape[1]
    ids = lax.broadcasted_iota(jnp.int32, (pairs, total_nodes), 1).astype(jnp.float32)
    pair_at = lax.broadcasted_iota(jnp.int32, (pairs, 1), 0)
    pair_step = pair_at // nodes
    current = (pair_at % nodes + me * nodes).astype(jnp.float32)
    places = [None] * steps
    for step in reversed(range(steps)):
        reached = pair_step >= step
        places[step] = jnp.where(reached, current, -1.0)
        parent = forks[step : step + 1, :]
        parent = jnp.where(parent >= 0.0, parent, ids)
        found = jnp.where(ids == current, parent, 0.0).sum(-1, keepdims=True)
        current = jnp.where(reached, found, current)
    lane = lax.broadcasted_iota(jnp.int32, (pairs, BLOCK), 1)
    wanted = jnp.broadcast_to(current, (pairs, BLOCK))
    for step in range(steps):
        wanted = jnp.where(
            lane >= pool_rows + step * nodes * kv_local, places[step], wanted
        )
    is_new = lane >= pool_rows
    new_node = ((lane - pool_rows) // kv_local % nodes).astype(jnp.float32)
    inside = lane < pool_rows + new_rows
    parity = lane % kv_local

    own_copy.wait()
    for copy in pack_copies:
        copy.wait()

    def tail_score(d, highest):
        s = lax.dot_general(
            q, packs[d, :BLOCK, :], contract, preferred_element_type=jnp.float32
        )
        node = packs[d, pool_rows + new_rows : pool_rows + new_rows + 16, :].astype(jnp.float32)
        node = jnp.where(is_new, new_node, jnp.broadcast_to(node[0:1, :], (pairs, BLOCK)))
        base = (d * nodes).astype(jnp.float32)
        seen = inside & (node >= 0.0) & (node + base == wanted)
        pieces = []
        for k in range(kv_local):
            keep = (seen & (parity == k))[None]
            part = s[k * group * pairs : (k + 1) * group * pairs].reshape(group, pairs, BLOCK)
            pieces.append(jnp.where(keep, part, -jnp.inf).reshape(group * pairs, BLOCK))
        s = jnp.concatenate(pieces, axis=0)
        tail_scores[d] = s
        return jnp.maximum(highest, s.max(-1, keepdims=True))

    highest = lax.fori_loop(0, dp, tail_score, prompt_max)
    carried = jnp.exp2((prompt_max - highest) * factor)

    def tail_weigh(d, carry):
        total, acc = carry
        w = jnp.exp2((tail_scores[d] - highest) * factor)
        total = total + w.sum(-1, keepdims=True)
        acc = acc + jnp.dot(
            w.astype(jnp.bfloat16), packs[d, BLOCK : 2 * BLOCK, :],
            preferred_element_type=jnp.float32,
        )
        return total, acc

    denominator, mixed = lax.fori_loop(
        0, dp, tail_weigh, (prompt_sum * carried, prompt_acc * carried)
    )
    attended = (mixed / denominator).astype(jnp.bfloat16)
    for h in range(head_count):
        heads[me, :, h * head_dim : (h + 1) * head_dim] = attended[h * pairs : (h + 1) * pairs]

    head_copies = []
    for hop in range(1, dp):
        copy = pltpu.make_async_remote_copy(
            src_ref=heads.at[me],
            dst_ref=heads.at[me],
            send_sem=head_send.at[hop],
            recv_sem=head_recv.at[hop],
            device_id={"dp": lax.rem(me + hop, dp)},
            device_id_type=MESH,
        )
        copy.start()
        head_copies.append(copy)
    weight_copy.wait()
    for copy in head_copies:
        copy.wait()

    columns = weight.shape[1]
    per_tensor = dp // tensor
    gathered = heads[...].reshape(dp * pairs, head_count * head_dim)
    part_copies = []
    for at in range(columns // tile):
        here = slice(at * tile, (at + 1) * tile)
        product = jnp.dot(gathered, weight[:, here], preferred_element_type=jnp.float32)
        partial[at] = product.astype(jnp.bfloat16).reshape(tensor, per_tensor * pairs, tile)
        for hop in range(1, tensor):
            peer = lax.rem(me_tensor + hop, tensor)
            copy = pltpu.make_async_remote_copy(
                src_ref=partial.at[at, peer],
                dst_ref=landed.at[at, hop],
                send_sem=part_send.at[at, hop],
                recv_sem=part_recv.at[at, hop],
                device_id={"tensor": peer},
                device_id_type=MESH,
            )
            copy.start()
            part_copies.append(copy)
    for at in range(columns // tile):
        here = slice(at * tile, (at + 1) * tile)
        for copy in part_copies[at * (tensor - 1) : (at + 1) * (tensor - 1)]:
            copy.wait()
        total = partial[at, me_tensor].astype(jnp.float32)
        for hop in range(1, tensor):
            total = total + landed[at, hop].astype(jnp.float32)
        out_ref[:, here] = (residual_ref[:, here].astype(jnp.float32) + total).astype(jnp.bfloat16)


def local(
    dp, tensor,
    query, new_kv, tail_pool, page_table, tail_len, fork_parent, prompt_kv, out_weight, residual,
):
    steps, nodes, head_count, head_dim = query.shape
    pages, page, kv_local, _ = tail_pool.shape
    prompt = prompt_kv.shape[0]
    columns = out_weight.shape[1]
    pairs = steps * nodes
    rows = pairs * head_count
    per_tensor = dp // tensor
    pool_rows = pages * page * kv_local
    new_rows = pairs * kv_local
    tile = min(512, columns)
    width = 1024
    chunks = prompt * kv_local // width
    bf16 = jnp.bfloat16

    keys = prompt_kv[..., :head_dim].reshape(prompt * kv_local, head_dim)
    values = prompt_kv[..., head_dim:].reshape(prompt * kv_local, head_dim)

    at_page = jnp.arange(pages, dtype=jnp.int32)
    match = page_table[:, :, None] == at_page
    table_node = jnp.arange(nodes, dtype=jnp.int32)[:, None, None]
    logical = jnp.arange(page_table.shape[1], dtype=jnp.int32)[None, :, None]
    owner = jnp.where(match, table_node, 0).sum((0, 1))
    filled = jnp.where(match, tail_len[:, None, None] - logical * page, 0).sum((0, 1))
    live = jnp.arange(page, dtype=jnp.int32)[None, :] < filled[:, None]
    node_row = jnp.where(live, owner[:, None], -1).astype(bf16)
    node_row = jnp.repeat(node_row.reshape(-1), kv_local)
    meta = jnp.broadcast_to(jnp.pad(node_row, (0, head_dim - pool_rows)), (16, head_dim))
    spare = BLOCK - pool_rows - new_rows
    pack = jnp.concatenate(
        [
            tail_pool[..., :head_dim].reshape(pool_rows, head_dim),
            new_kv[..., :head_dim].reshape(new_rows, head_dim),
            meta,
            jnp.zeros((spare - 16, head_dim), bf16),
            tail_pool[..., head_dim:].reshape(pool_rows, head_dim),
            new_kv[..., head_dim:].reshape(new_rows, head_dim),
            jnp.zeros((spare, head_dim), bf16),
        ]
    )
    residual_rows = (
        residual.reshape(steps, per_tensor, nodes, columns)
        .transpose(1, 0, 2, 3)
        .reshape(per_tensor * pairs, columns)
    )

    dims = (dp, tensor, steps, nodes, head_count, kv_local, head_dim, pages, page, tile)
    vmem = pl.BlockSpec(memory_space=pltpu.VMEM)
    tiles = columns // tile
    dma = pltpu.SemaphoreType.DMA
    out = pl.pallas_call(
        functools.partial(kernel, dims),
        out_shape=jax.ShapeDtypeStruct((per_tensor * pairs, columns), bf16),
        in_specs=[vmem] * 5 + [pl.BlockSpec(memory_space=pl.ANY), vmem],
        out_specs=vmem,
        scratch_shapes=[
            pltpu.VMEM((rows, head_dim), jnp.float32),
            pltpu.VMEM((chunks, rows, width), jnp.float32),
            pltpu.VMEM((dp, rows, BLOCK), jnp.float32),
            pltpu.VMEM((dp, 2 * BLOCK, head_dim), bf16),
            pltpu.VMEM(out_weight.shape, bf16),
            pltpu.VMEM((dp, pairs, head_count * head_dim), bf16),
            pltpu.VMEM((tiles, tensor, per_tensor * pairs, tile), bf16),
            pltpu.VMEM((tiles, tensor, per_tensor * pairs, tile), bf16),
            dma,
            dma,
            dma((dp,)),
            dma((dp,)),
            dma((dp,)),
            dma((dp,)),
            dma((tiles, tensor)),
            dma((tiles, tensor)),
        ],
        compiler_params=pltpu.CompilerParams(
            collective_id=0, has_side_effects=True, vmem_limit_bytes=48 * 1024 * 1024
        ),
    )(
        query.reshape(rows, head_dim), keys, values, pack, fork_parent, out_weight, residual_rows
    )
    return (
        out.reshape(per_tensor, steps, nodes, columns)
        .transpose(1, 0, 2, 3)
        .reshape(residual.shape)
    )


def solution(mesh):
    in_specs = (
        P(None, ("groups", "dp"), "tensor", None),
        P(None, ("groups", "dp"), "tensor", None),
        P(("groups", "dp"), None, "tensor", None),
        P(("groups", "dp"), None),
        P(("groups", "dp")),
        P(None, "groups"),
        P("groups", "tensor", None),
        P("tensor", "dp"),
        P(None, ("groups", "tensor"), "dp"),
    )
    out_specs = P(None, ("groups", "tensor"), "dp")
    body = functools.partial(local, mesh.shape["dp"], mesh.shape["tensor"])
    return jax.shard_map(body, mesh=mesh, in_specs=in_specs, out_specs=out_specs, check_vma=False)
```

```python
import functools
import math

import jax
import jax.numpy as jnp
from jax import lax
from jax.experimental import pallas as pl
from jax.experimental.pallas import tpu as pltpu
from jax.sharding import PartitionSpec as P

MESH = pl.DeviceIdType.MESH
BLOCK = 128


def kernel(
    dims, table_ref, len_ref, q_ref, fork_ref, residual_ref, prompt_ref, pool_ref, new_ref,
    weight_ref, out_ref,
    q_flat, prompt_keys, prompt_values, scores, tail_scores, packs, owners, weight, heads,
    partial, landed,
    weight_sem, own_sem, prompt_sem, pack_send, pack_recv, owner_send, owner_recv,
    head_send, head_recv, part_send, part_recv,
):
    dp, tensor, steps, nodes, head_count, kv_local, head_dim, pages, page, tile = dims
    pairs = steps * nodes
    rows = pairs * head_count
    group = head_count // kv_local
    pool_rows = pages * page * kv_local
    new_rows = pairs * kv_local
    me = lax.axis_index("dp")
    me_tensor = lax.axis_index("tensor")
    factor = head_dim ** (-0.5) * math.log2(math.e)

    total_chunks, chunk_prompt = prompt_keys.shape[0], prompt_keys.shape[1]
    pool_tokens = pages * page
    half = BLOCK // kv_local

    own_copies = []
    for part in range(2):
        lanes = slice(part * head_dim, (part + 1) * head_dim)
        own_copies.append(
            pltpu.make_async_copy(
                pool_ref.at[:, :, lanes], packs.at[me, part, 0:pool_tokens], own_sem.at[part, 0]
            )
        )
        own_copies.append(
            pltpu.make_async_copy(
                new_ref.at[:, :, lanes], packs.at[me, part, pool_tokens : pool_tokens + pairs],
                own_sem.at[part, 1],
            )
        )
    for copy in own_copies:
        copy.start()

    def prompt_copy(c, part):
        return pltpu.make_async_copy(
            prompt_ref.at[
                pl.ds(c * chunk_prompt, chunk_prompt), :,
                part * head_dim : (part + 1) * head_dim,
            ],
            (prompt_values if part else prompt_keys).at[c],
            prompt_sem.at[part, c],
        )

    for part in range(2):
        for c in range(total_chunks):
            prompt_copy(c, part).start()
    weight_copy = pltpu.make_async_copy(weight_ref, weight, weight_sem)
    weight_copy.start()

    barrier = pltpu.get_barrier_semaphore()
    for hop in range(1, dp):
        pl.semaphore_signal(
            barrier, inc=1, device_id={"dp": lax.rem(me + hop, dp)}, device_id_type=MESH
        )
    for hop in range(1, tensor):
        pl.semaphore_signal(
            barrier, inc=1, device_id={"tensor": lax.rem(me_tensor + hop, tensor)},
            device_id_type=MESH,
        )

    spot = lax.broadcasted_iota(jnp.int32, (16, BLOCK), 1) // kv_local
    owner = jnp.full((16, BLOCK), -1.0, jnp.float32)
    for n in range(nodes):
        for j in range(pages // nodes):
            held = (spot // page == table_ref[j, n]) & (spot % page + j * page < len_ref[n])
            owner = jnp.where(held & (spot < pool_tokens), float(n), owner)
    owners[me] = owner.astype(jnp.bfloat16)
    used = pool_tokens + pairs
    for part in range(2):
        packs[me, part, used:half] = jnp.zeros(
            (half - used, kv_local, head_dim), jnp.bfloat16
        )
    for copy in own_copies:
        copy.wait()
    pl.semaphore_wait(barrier, dp + tensor - 2)

    pack_copies = []
    for hop in range(1, dp):
        for buffer, send, recv in (
            (packs, pack_send, pack_recv), (owners, owner_send, owner_recv)
        ):
            copy = pltpu.make_async_remote_copy(
                src_ref=buffer.at[me],
                dst_ref=buffer.at[me],
                send_sem=send.at[hop],
                recv_sem=recv.at[hop],
                device_id={"dp": lax.rem(me + hop, dp)},
                device_id_type=MESH,
            )
            copy.start()
            pack_copies.append(copy)

    q_flat[...] = q_ref[...].astype(jnp.float32)
    q = jnp.concatenate(
        [q_flat[pl.ds(h, pairs, stride=head_count), :] for h in range(head_count)], axis=0
    ).astype(jnp.bfloat16)
    contract = (((1,), (1,)), ((), ()))

    width = scores.shape[2]
    chunks = scores.shape[0]
    row_kv = lax.broadcasted_iota(jnp.int32, (rows, width), 0) // (group * pairs)
    col_kv = lax.broadcasted_iota(jnp.int32, (rows, width), 1) % kv_local
    same = row_kv == col_kv

    def score_chunk(c, highest):
        prompt_copy(c, 0).wait()
        s = lax.dot_general(
            q, prompt_keys.at[c].reshape(width, head_dim)[...], contract, preferred_element_type=jnp.float32
        )
        s = jnp.where(same, s, -jnp.inf)
        scores[c] = s
        return jnp.maximum(highest, s.max(-1, keepdims=True))

    prompt_max = lax.fori_loop(
        0, chunks, score_chunk, jnp.full((rows, 1), -jnp.inf, jnp.float32)
    )

    def weigh_chunk(c, carry):
        total, acc = carry
        prompt_copy(c, 1).wait()
        w = jnp.exp2((scores[c] - prompt_max) * factor)
        total = total + w.sum(-1, keepdims=True)
        acc = acc + jnp.dot(
            w.astype(jnp.bfloat16), prompt_values.at[c].reshape(width, head_dim)[...],
            preferred_element_type=jnp.float32,
        )
        return total, acc

    prompt_sum, prompt_acc = lax.fori_loop(
        0, chunks, weigh_chunk,
        (jnp.zeros((rows, 1), jnp.float32), jnp.zeros((rows, head_dim), jnp.float32)),
    )

    forks = fork_ref[...].astype(jnp.float32)
    total_nodes = forks.shape[1]
    ids = lax.broadcasted_iota(jnp.int32, (pairs, total_nodes), 1).astype(jnp.float32)
    pair_at = lax.broadcasted_iota(jnp.int32, (pairs, 1), 0)
    pair_step = pair_at // nodes
    current = (pair_at % nodes + me * nodes).astype(jnp.float32)
    places = [None] * steps
    for step in reversed(range(steps)):
        reached = pair_step >= step
        places[step] = jnp.where(reached, current, -1.0)
        parent = forks[step : step + 1, :]
        parent = jnp.where(parent >= 0.0, parent, ids)
        found = jnp.where(ids == current, parent, 0.0).sum(-1, keepdims=True)
        current = jnp.where(reached, found, current)
    lane = lax.broadcasted_iota(jnp.int32, (pairs, BLOCK), 1)
    wanted = jnp.broadcast_to(current, (pairs, BLOCK))
    for step in range(steps):
        wanted = jnp.where(
            lane >= pool_rows + step * nodes * kv_local, places[step], wanted
        )
    is_new = lane >= pool_rows
    new_node = ((lane - pool_rows) // kv_local % nodes).astype(jnp.float32)
    inside = lane < pool_rows + new_rows
    parity = lane % kv_local

    for copy in pack_copies:
        copy.wait()

    def tail_score(d, highest):
        s = lax.dot_general(
            q, packs.at[d, 0].reshape(BLOCK, head_dim)[...], contract, preferred_element_type=jnp.float32
        )
        node = owners[d].astype(jnp.float32)
        node = jnp.where(is_new, new_node, jnp.broadcast_to(node[0:1, :], (pairs, BLOCK)))
        base = (d * nodes).astype(jnp.float32)
        seen = inside & (node >= 0.0) & (node + base == wanted)
        pieces = []
        for k in range(kv_local):
            keep = (seen & (parity == k))[None]
            part = s[k * group * pairs : (k + 1) * group * pairs].reshape(group, pairs, BLOCK)
            pieces.append(jnp.where(keep, part, -jnp.inf).reshape(group * pairs, BLOCK))
        s = jnp.concatenate(pieces, axis=0)
        tail_scores[d] = s
        return jnp.maximum(highest, s.max(-1, keepdims=True))

    highest = lax.fori_loop(0, dp, tail_score, prompt_max)
    carried = jnp.exp2((prompt_max - highest) * factor)

    def tail_weigh(d, carry):
        total, acc = carry
        w = jnp.exp2((tail_scores[d] - highest) * factor)
        total = total + w.sum(-1, keepdims=True)
        acc = acc + jnp.dot(
            w.astype(jnp.bfloat16), packs.at[d, 1].reshape(BLOCK, head_dim)[...],
            preferred_element_type=jnp.float32,
        )
        return total, acc

    denominator, mixed = lax.fori_loop(
        0, dp, tail_weigh, (prompt_sum * carried, prompt_acc * carried)
    )
    attended = (mixed / denominator).astype(jnp.bfloat16)
    for h in range(head_count):
        heads[me, :, h * head_dim : (h + 1) * head_dim] = attended[h * pairs : (h + 1) * pairs]

    head_copies = []
    for hop in range(1, dp):
        copy = pltpu.make_async_remote_copy(
            src_ref=heads.at[me],
            dst_ref=heads.at[me],
            send_sem=head_send.at[hop],
            recv_sem=head_recv.at[hop],
            device_id={"dp": lax.rem(me + hop, dp)},
            device_id_type=MESH,
        )
        copy.start()
        head_copies.append(copy)
    weight_copy.wait()
    for copy in head_copies:
        copy.wait()

    columns = weight.shape[1]
    per_tensor = dp // tensor
    gathered = heads[...].reshape(dp * pairs, head_count * head_dim)
    part_copies = []
    for at in range(columns // tile):
        here = slice(at * tile, (at + 1) * tile)
        product = jnp.dot(gathered, weight[:, here], preferred_element_type=jnp.float32)
        partial[at] = product.astype(jnp.bfloat16).reshape(tensor, per_tensor * pairs, tile)
        for hop in range(1, tensor):
            peer = lax.rem(me_tensor + hop, tensor)
            copy = pltpu.make_async_remote_copy(
                src_ref=partial.at[at, peer],
                dst_ref=landed.at[at, hop],
                send_sem=part_send.at[at, hop],
                recv_sem=part_recv.at[at, hop],
                device_id={"tensor": peer},
                device_id_type=MESH,
            )
            copy.start()
            part_copies.append(copy)
    for at in range(columns // tile):
        here = slice(at * tile, (at + 1) * tile)
        for copy in part_copies[at * (tensor - 1) : (at + 1) * (tensor - 1)]:
            copy.wait()
        total = partial[at, me_tensor].astype(jnp.float32)
        for hop in range(1, tensor):
            total = total + landed[at, hop].astype(jnp.float32)
        for s in range(steps):
            for block in range(per_tensor):
                own = slice(block * nodes, (block + 1) * nodes)
                at_row = block * pairs + s * nodes
                out_ref[s, own, here] = (
                    residual_ref[s, own, here].astype(jnp.float32)
                    + total[at_row : at_row + nodes]
                ).astype(jnp.bfloat16)


def local(
    dp, tensor,
    query, new_kv, tail_pool, page_table, tail_len, fork_parent, prompt_kv, out_weight, residual,
):
    steps, nodes, head_count, head_dim = query.shape
    pages, page, kv_local, _ = tail_pool.shape
    prompt = prompt_kv.shape[0]
    columns = out_weight.shape[1]
    pairs = steps * nodes
    rows = pairs * head_count
    per_tensor = dp // tensor
    tile = min(512, columns)
    width = 1024
    chunks = prompt * kv_local // width
    bf16 = jnp.bfloat16

    dims = (dp, tensor, steps, nodes, head_count, kv_local, head_dim, pages, page, tile)
    vmem = pl.BlockSpec(memory_space=pltpu.VMEM)
    tiles = columns // tile
    dma = pltpu.SemaphoreType.DMA
    return pl.pallas_call(
        functools.partial(kernel, dims),
        out_shape=jax.ShapeDtypeStruct(residual.shape, bf16),
        in_specs=[pl.BlockSpec(memory_space=pltpu.SMEM)] * 2
        + [vmem] * 3
        + [pl.BlockSpec(memory_space=pltpu.HBM)] * 4,
        out_specs=vmem,
        scratch_shapes=[
            pltpu.VMEM((rows, head_dim), jnp.float32),
            pltpu.VMEM((chunks, width // kv_local, kv_local, head_dim), bf16),
            pltpu.VMEM((chunks, width // kv_local, kv_local, head_dim), bf16),
            pltpu.VMEM((chunks, rows, width), jnp.float32),
            pltpu.VMEM((dp, rows, BLOCK), jnp.float32),
            pltpu.VMEM((dp, 2, BLOCK // kv_local, kv_local, head_dim), bf16),
            pltpu.VMEM((dp, 16, BLOCK), bf16),
            pltpu.VMEM(out_weight.shape, bf16),
            pltpu.VMEM((dp, pairs, head_count * head_dim), bf16),
            pltpu.VMEM((tiles, tensor, per_tensor * pairs, tile), bf16),
            pltpu.VMEM((tiles, tensor, per_tensor * pairs, tile), bf16),
            dma,
            dma((2, 2)),
            dma((2, chunks)),
            dma((dp,)),
            dma((dp,)),
            dma((dp,)),
            dma((dp,)),
            dma((dp,)),
            dma((dp,)),
            dma((tiles, tensor)),
            dma((tiles, tensor)),
        ],
        compiler_params=pltpu.CompilerParams(
            collective_id=0, has_side_effects=True, vmem_limit_bytes=63 * 1024 * 1024
        ),
    )(
        page_table.T,
        tail_len,
        query.reshape(rows, head_dim),
        fork_parent,
        residual,
        prompt_kv,
        tail_pool.reshape(pages * page, kv_local, 2 * head_dim),
        new_kv.reshape(pairs, kv_local, 2 * head_dim),
        out_weight,
    )


def solution(mesh):
    in_specs = (
        P(None, ("groups", "dp"), "tensor", None),
        P(None, ("groups", "dp"), "tensor", None),
        P(("groups", "dp"), None, "tensor", None),
        P(("groups", "dp"), None),
        P(("groups", "dp")),
        P(None, "groups"),
        P("groups", "tensor", None),
        P("tensor", "dp"),
        P(None, ("groups", "tensor"), "dp"),
    )
    out_specs = P(None, ("groups", "tensor"), "dp")
    body = functools.partial(local, mesh.shape["dp"], mesh.shape["tensor"])
    return jax.shard_map(body, mesh=mesh, in_specs=in_specs, out_specs=out_specs, check_vma=False)
```

```python
import functools
import math

import jax
import jax.numpy as jnp
from jax import lax
from jax.experimental import pallas as pl
from jax.experimental.pallas import tpu as pltpu
from jax.sharding import PartitionSpec as P

MESH = pl.DeviceIdType.MESH
BLOCK = 128
TAIL_WIDTH = 256


def kernel(
    dims, table_in, len_in, q_in, fork_in, residual_in, pool_in, prompt_ref, new_ref,
    weight_ref, out_ref,
    table_ref, len_ref, q_ref, fork_ref, residual_ref, pool_ref,
    q_flat, prompt_keys, prompt_values, scores, tail_scores, packs, owners, weight, heads,
    partial, landed,
    in_sem, weight_sem, own_sem, prompt_sem, pack_send, pack_recv, owner_send, owner_recv,
    head_send, head_recv, part_send, part_recv,
):
    dp, tensor, steps, nodes, head_count, kv_local, head_dim, pages, page, tile = dims
    pairs = steps * nodes
    rows = pairs * head_count
    group = head_count // kv_local
    pool_rows = pages * page * kv_local
    new_rows = pairs * kv_local
    me = lax.axis_index("dp")
    me_tensor = lax.axis_index("tensor")
    factor = head_dim ** (-0.5) * math.log2(math.e)

    total_chunks, chunk_prompt = prompt_keys.shape[0], prompt_keys.shape[1]
    pool_tokens = nodes * page
    span = (pool_tokens + pairs) * kv_local
    join = TAIL_WIDTH // span

    small_copies = [
        pltpu.make_async_copy(source, target, in_sem.at[at])
        for at, (source, target) in enumerate(
            (
                (table_in, table_ref), (len_in, len_ref), (pool_in, pool_ref), (q_in, q_ref),
                (fork_in, fork_ref), (residual_in, residual_ref),
            )
        )
    ]
    for copy in small_copies[:3]:
        copy.start()
    own_copies = []
    for part in range(2):
        lanes = slice(part * head_dim, (part + 1) * head_dim)
        own_copies.append(
            pltpu.make_async_copy(
                new_ref.at[:, :, lanes], packs.at[part, me, pool_tokens : pool_tokens + pairs],
                own_sem.at[part],
            )
        )
    for copy in own_copies + small_copies[3:]:
        copy.start()

    def prompt_copy(c, part):
        return pltpu.make_async_copy(
            prompt_ref.at[
                pl.ds(c * chunk_prompt, chunk_prompt), :,
                part * head_dim : (part + 1) * head_dim,
            ],
            (prompt_values if part else prompt_keys).at[c],
            prompt_sem.at[part, c],
        )

    for part in range(2):
        for c in range(total_chunks):
            prompt_copy(c, part).start()
    weight_copy = pltpu.make_async_copy(weight_ref, weight, weight_sem)
    weight_copy.start()

    barrier = pltpu.get_barrier_semaphore()
    for hop in range(1, dp):
        pl.semaphore_signal(
            barrier, inc=1, device_id={"dp": lax.rem(me + hop, dp)}, device_id_type=MESH
        )
    for hop in range(1, tensor):
        pl.semaphore_signal(
            barrier, inc=1, device_id={"tensor": lax.rem(me_tensor + hop, tensor)},
            device_id_type=MESH,
        )

    for copy in small_copies[:3]:
        copy.wait()
    lane = lax.broadcasted_iota(jnp.int32, (16, BLOCK), 1)
    spot = lane % span // kv_local
    owner = (spot - pool_tokens) % nodes
    for n in range(nodes):
        owner = jnp.where(
            spot // page == n, jnp.where(spot % page < len_ref[n], n, -1 - me * nodes), owner
        )
        for part in range(2):
            lanes = slice(part * head_dim, (part + 1) * head_dim)
            packs[part, me, n * page : (n + 1) * page] = pool_ref[table_ref[0, n], :, :, lanes]
    owner = jnp.where(lane // span == me % (BLOCK // span), owner + me * nodes, -1)
    owners[me] = owner.astype(jnp.float32).astype(jnp.bfloat16)
    for copy in own_copies:
        copy.wait()
    pl.semaphore_wait(barrier, dp + tensor - 2)

    pack_copies = []
    for hop in range(1, dp):
        for buffer, send, recv in (
            (owners.at[me], owner_send.at[hop], owner_recv.at[hop]),
            (packs.at[0, me], pack_send.at[0, hop], pack_recv.at[0, hop]),
            (packs.at[1, me], pack_send.at[1, hop], pack_recv.at[1, hop]),
        ):
            copy = pltpu.make_async_remote_copy(
                src_ref=buffer,
                dst_ref=buffer,
                send_sem=send,
                recv_sem=recv,
                device_id={"dp": lax.rem(me + hop, dp)},
                device_id_type=MESH,
            )
            copy.start()
            pack_copies.append(copy)

    for copy in small_copies[3:]:
        copy.wait()
    q_flat[...] = q_ref[...].astype(jnp.float32)
    q = jnp.concatenate(
        [q_flat[pl.ds(h, pairs, stride=head_count), :] for h in range(head_count)], axis=0
    ).astype(jnp.bfloat16)
    contract = (((1,), (1,)), ((), ()))

    width = scores.shape[2]
    chunks = scores.shape[0]
    row_kv = lax.broadcasted_iota(jnp.int32, (rows, width), 0) // (group * pairs)
    col_kv = lax.broadcasted_iota(jnp.int32, (rows, width), 1) % kv_local
    same = row_kv == col_kv

    def score_chunk(c, highest):
        prompt_copy(c, 0).wait()
        s = lax.dot_general(
            q, prompt_keys.at[c].reshape(width, head_dim)[...], contract, preferred_element_type=jnp.float32
        )
        s = jnp.where(same, s, -jnp.inf)
        scores[c] = s
        return jnp.maximum(highest, s.max(-1, keepdims=True))

    prompt_max = lax.fori_loop(
        0, chunks, score_chunk, jnp.full((rows, 1), -jnp.inf, jnp.float32)
    )

    def weigh_chunk(c, carry):
        total, acc = carry
        prompt_copy(c, 1).wait()
        w = jnp.exp2((scores[c] - prompt_max) * factor)
        total = total + w.sum(-1, keepdims=True)
        acc = acc + jnp.dot(
            w.astype(jnp.bfloat16), prompt_values.at[c].reshape(width, head_dim)[...],
            preferred_element_type=jnp.float32,
        )
        return total, acc

    prompt_sum, prompt_acc = lax.fori_loop(
        0, chunks, weigh_chunk,
        (jnp.zeros((rows, 1), jnp.float32), jnp.zeros((rows, head_dim), jnp.float32)),
    )

    forks = fork_ref[...].astype(jnp.float32)
    total_nodes = forks.shape[1]
    ids = lax.broadcasted_iota(jnp.int32, (pairs, total_nodes), 1).astype(jnp.float32)
    pair_at = lax.broadcasted_iota(jnp.int32, (pairs, 1), 0)
    pair_step = pair_at // nodes
    current = (pair_at % nodes + me * nodes).astype(jnp.float32)
    places = [None] * steps
    for step in reversed(range(steps)):
        reached = pair_step >= step
        places[step] = jnp.where(reached, current, -1.0)
        parent = forks[step : step + 1, :]
        parent = jnp.where(parent >= 0.0, parent, ids)
        found = jnp.where(ids == current, parent, 0.0).sum(-1, keepdims=True)
        current = jnp.where(reached, found, current)
    lane = lax.broadcasted_iota(jnp.int32, (pairs, TAIL_WIDTH), 1)
    spot = lane % span // kv_local
    wanted = jnp.broadcast_to(current, (pairs, TAIL_WIDTH))
    for step in range(steps):
        wanted = jnp.where(spot >= pool_tokens + step * nodes, places[step], wanted)
    parity = lane % kv_local
    reachable = wanted >= 0.0

    for copy in pack_copies:
        copy.wait()

    def tail_keys(part, d):
        return packs.at[part, pl.ds(d * join, join)].reshape(TAIL_WIDTH, head_dim)[...]

    def tail_score(d, highest):
        s = lax.dot_general(
            q, tail_keys(0, d), contract, preferred_element_type=jnp.float32
        )
        per_block = BLOCK // span
        blocks = []
        for first in range(0, join, per_block):
            node = owners[d * join + first].astype(jnp.float32)
            for more in range(first + 1, first + per_block):
                node = jnp.maximum(node, owners[d * join + more].astype(jnp.float32))
            blocks.append(node)
        node = jnp.concatenate(blocks, axis=1)[0:1, :]
        seen = reachable & (node == wanted)
        pieces = []
        for k in range(kv_local):
            keep = (seen & (parity == k))[None]
            part = s[k * group * pairs : (k + 1) * group * pairs].reshape(group, pairs, TAIL_WIDTH)
            pieces.append(jnp.where(keep, part, -jnp.inf).reshape(group * pairs, TAIL_WIDTH))
        s = jnp.concatenate(pieces, axis=0)
        tail_scores[d] = s
        return jnp.maximum(highest, s.max(-1, keepdims=True))

    highest = lax.fori_loop(0, dp // join, tail_score, prompt_max)
    carried = jnp.exp2((prompt_max - highest) * factor)

    def tail_weigh(d, carry):
        total, acc = carry
        w = jnp.exp2((tail_scores[d] - highest) * factor)
        total = total + w.sum(-1, keepdims=True)
        acc = acc + jnp.dot(
            w.astype(jnp.bfloat16), tail_keys(1, d),
            preferred_element_type=jnp.float32,
        )
        return total, acc

    denominator, mixed = lax.fori_loop(
        0, dp // join, tail_weigh, (prompt_sum * carried, prompt_acc * carried)
    )
    attended = (mixed / denominator).astype(jnp.bfloat16)
    for h in range(head_count):
        heads[me, :, h * head_dim : (h + 1) * head_dim] = attended[h * pairs : (h + 1) * pairs]

    head_copies = []
    for hop in range(1, dp):
        copy = pltpu.make_async_remote_copy(
            src_ref=heads.at[me],
            dst_ref=heads.at[me],
            send_sem=head_send.at[hop],
            recv_sem=head_recv.at[hop],
            device_id={"dp": lax.rem(me + hop, dp)},
            device_id_type=MESH,
        )
        copy.start()
        head_copies.append(copy)
    weight_copy.wait()
    for copy in head_copies:
        copy.wait()

    columns = weight.shape[1]
    per_tensor = dp // tensor
    gathered = heads[...].reshape(dp * pairs, head_count * head_dim)
    part_copies = []
    for at in range(columns // tile):
        here = slice(at * tile, (at + 1) * tile)
        product = jnp.dot(gathered, weight[:, here], preferred_element_type=jnp.float32)
        partial[at] = product.astype(jnp.bfloat16).reshape(tensor, per_tensor * pairs, tile)
        for hop in range(1, tensor):
            peer = lax.rem(me_tensor + hop, tensor)
            copy = pltpu.make_async_remote_copy(
                src_ref=partial.at[at, peer],
                dst_ref=landed.at[at, hop],
                send_sem=part_send.at[at, hop],
                recv_sem=part_recv.at[at, hop],
                device_id={"tensor": peer},
                device_id_type=MESH,
            )
            copy.start()
            part_copies.append(copy)
    for at in range(columns // tile):
        here = slice(at * tile, (at + 1) * tile)
        for copy in part_copies[at * (tensor - 1) : (at + 1) * (tensor - 1)]:
            copy.wait()
        total = partial[at, me_tensor].astype(jnp.float32)
        for hop in range(1, tensor):
            total = total + landed[at, hop].astype(jnp.float32)
        for s in range(steps):
            for block in range(per_tensor):
                own = slice(block * nodes, (block + 1) * nodes)
                at_row = block * pairs + s * nodes
                out_ref[s, own, here] = (
                    residual_ref[s, own, here].astype(jnp.float32)
                    + total[at_row : at_row + nodes]
                ).astype(jnp.bfloat16)


def local(
    dp, tensor,
    query, new_kv, tail_pool, page_table, tail_len, fork_parent, prompt_kv, out_weight, residual,
):
    steps, nodes, head_count, head_dim = query.shape
    pages, page, kv_local, _ = tail_pool.shape
    prompt = prompt_kv.shape[0]
    columns = out_weight.shape[1]
    pairs = steps * nodes
    rows = pairs * head_count
    per_tensor = dp // tensor
    span = (nodes * page + pairs) * kv_local
    tile = min(512, columns)
    width = 1024
    chunks = prompt * kv_local // width
    bf16 = jnp.bfloat16

    dims = (dp, tensor, steps, nodes, head_count, kv_local, head_dim, pages, page, tile)
    vmem = pl.BlockSpec(memory_space=pltpu.VMEM)
    tiles = columns // tile
    dma = pltpu.SemaphoreType.DMA
    return pl.pallas_call(
        functools.partial(kernel, dims),
        out_shape=jax.ShapeDtypeStruct(residual.shape, bf16),
        in_specs=[pl.BlockSpec(memory_space=pltpu.HBM)] * 9,
        out_specs=vmem,
        scratch_shapes=[
            pltpu.SMEM(page_table.shape[::-1], jnp.int32),
            pltpu.SMEM(tail_len.shape, jnp.int32),
            pltpu.VMEM((rows, head_dim), bf16),
            pltpu.VMEM(fork_parent.shape, jnp.int32),
            pltpu.VMEM(residual.shape, bf16),
            pltpu.VMEM(tail_pool.shape, bf16),
            pltpu.VMEM((rows, head_dim), jnp.float32),
            pltpu.VMEM((chunks, width // kv_local, kv_local, head_dim), bf16),
            pltpu.VMEM((chunks, width // kv_local, kv_local, head_dim), bf16),
            pltpu.VMEM((chunks, rows, width), jnp.float32),
            pltpu.VMEM((dp * span // TAIL_WIDTH, rows, TAIL_WIDTH), jnp.float32),
            pltpu.VMEM((2, dp, span // kv_local, kv_local, head_dim), bf16),
            pltpu.VMEM((dp, 16, BLOCK), bf16),
            pltpu.VMEM(out_weight.shape, bf16),
            pltpu.VMEM((dp, pairs, head_count * head_dim), bf16),
            pltpu.VMEM((tiles, tensor, per_tensor * pairs, tile), bf16),
            pltpu.VMEM((tiles, tensor, per_tensor * pairs, tile), bf16),
            dma((6,)),
            dma,
            dma((2,)),
            dma((2, chunks)),
            dma((2, dp)),
            dma((2, dp)),
            dma((dp,)),
            dma((dp,)),
            dma((dp,)),
            dma((dp,)),
            dma((tiles, tensor)),
            dma((tiles, tensor)),
        ],
        compiler_params=pltpu.CompilerParams(
            collective_id=0, has_side_effects=True, vmem_limit_bytes=63 * 1024 * 1024
        ),
    )(
        page_table.T,
        tail_len,
        query.reshape(rows, head_dim),
        fork_parent,
        residual,
        tail_pool,
        prompt_kv,
        new_kv.reshape(pairs, kv_local, 2 * head_dim),
        out_weight,
    )


def solution(mesh):
    in_specs = (
        P(None, ("groups", "dp"), "tensor", None),
        P(None, ("groups", "dp"), "tensor", None),
        P(("groups", "dp"), None, "tensor", None),
        P(("groups", "dp"), None),
        P(("groups", "dp")),
        P(None, "groups"),
        P("groups", "tensor", None),
        P("tensor", "dp"),
        P(None, ("groups", "tensor"), "dp"),
    )
    out_specs = P(None, ("groups", "tensor"), "dp")
    body = functools.partial(local, mesh.shape["dp"], mesh.shape["tensor"])
    return jax.shard_map(body, mesh=mesh, in_specs=in_specs, out_specs=out_specs, check_vma=False)
```

```python
import functools
import math

import jax
import jax.numpy as jnp
from jax import lax
from jax.experimental import pallas as pl
from jax.experimental.pallas import tpu as pltpu
from jax.sharding import PartitionSpec as P

MESH = pl.DeviceIdType.MESH
BLOCK = 128
TAIL_WIDTH = 256


def kernel(
    dims, table_in, len_in, q_in, fork_in, residual_in, pool_in, prompt_ref, new_ref,
    weight_ref, out_ref,
    table_ref, len_ref, q_ref, fork_ref, residual_ref, pool_ref,
    q_flat, prompt_keys, prompt_values, scores, tail_scores, packs, owners, weight, heads,
    partial, landed,
    in_sem, weight_sem, own_sem, prompt_sem, pack_send, pack_recv, owner_send, owner_recv,
    head_send, head_recv, part_send, part_recv,
):
    dp, tensor, steps, nodes, head_count, kv_local, head_dim, pages, page, tile = dims
    pairs = steps * nodes
    rows = pairs * head_count
    group = head_count // kv_local
    pool_rows = pages * page * kv_local
    new_rows = pairs * kv_local
    me = lax.axis_index("dp")
    me_tensor = lax.axis_index("tensor")
    factor = head_dim ** (-0.5) * math.log2(math.e)

    total_chunks, chunk_prompt = prompt_keys.shape[0], prompt_keys.shape[1]
    pool_tokens = nodes * page
    span = (pool_tokens + pairs) * kv_local
    join = TAIL_WIDTH // span

    small_copies = [
        pltpu.make_async_copy(source, target, in_sem.at[at])
        for at, (source, target) in enumerate(
            (
                (table_in, table_ref), (len_in, len_ref), (pool_in, pool_ref), (q_in, q_ref),
                (fork_in, fork_ref), (residual_in, residual_ref),
            )
        )
    ]
    for copy in small_copies[:3]:
        copy.start()
    own_copies = []
    for part in range(2):
        lanes = slice(part * head_dim, (part + 1) * head_dim)
        own_copies.append(
            pltpu.make_async_copy(
                new_ref.at[:, :, lanes], packs.at[part, me, pool_tokens : pool_tokens + pairs],
                own_sem.at[part],
            )
        )
    for copy in own_copies + small_copies[3:]:
        copy.start()

    def prompt_copy(c, part):
        return pltpu.make_async_copy(
            prompt_ref.at[
                pl.ds(c * chunk_prompt, chunk_prompt), :,
                part * head_dim : (part + 1) * head_dim,
            ],
            (prompt_values if part else prompt_keys).at[c],
            prompt_sem.at[part, c],
        )

    for part in range(2):
        for c in range(total_chunks):
            prompt_copy(c, part).start()
    weight_copy = pltpu.make_async_copy(weight_ref, weight, weight_sem)
    weight_copy.start()

    barrier = pltpu.get_barrier_semaphore()
    for hop in range(1, dp):
        pl.semaphore_signal(
            barrier, inc=1, device_id={"dp": lax.rem(me + hop, dp)}, device_id_type=MESH
        )
    for hop in range(1, tensor):
        pl.semaphore_signal(
            barrier, inc=1, device_id={"tensor": lax.rem(me_tensor + hop, tensor)},
            device_id_type=MESH,
        )

    for copy in small_copies[:3]:
        copy.wait()
    lane = lax.broadcasted_iota(jnp.int32, (16, BLOCK), 1)
    spot = lane % span // kv_local
    owner = (spot - pool_tokens) % nodes
    for n in range(nodes):
        owner = jnp.where(
            spot // page == n, jnp.where(spot % page < len_ref[n], n, -1 - me * nodes), owner
        )
        for part in range(2):
            lanes = slice(part * head_dim, (part + 1) * head_dim)
            packs[part, me, n * page : (n + 1) * page] = pool_ref[table_ref[0, n], :, :, lanes]
    owner = jnp.where(lane // span == me % (BLOCK // span), owner + me * nodes, -1)
    owners[me] = owner.astype(jnp.float32).astype(jnp.bfloat16)
    for copy in own_copies:
        copy.wait()
    pl.semaphore_wait(barrier, dp + tensor - 2)

    pack_copies = []
    for hop in range(1, dp):
        for buffer, send, recv in (
            (owners.at[me], owner_send.at[hop], owner_recv.at[hop]),
            (packs.at[0, me], pack_send.at[0, hop], pack_recv.at[0, hop]),
            (packs.at[1, me], pack_send.at[1, hop], pack_recv.at[1, hop]),
        ):
            copy = pltpu.make_async_remote_copy(
                src_ref=buffer,
                dst_ref=buffer,
                send_sem=send,
                recv_sem=recv,
                device_id={"dp": lax.rem(me + hop, dp)},
                device_id_type=MESH,
            )
            copy.start()
            pack_copies.append(copy)

    for copy in small_copies[3:]:
        copy.wait()
    q_flat[...] = q_ref[...].astype(jnp.float32)
    q = jnp.concatenate(
        [q_flat[pl.ds(h, pairs, stride=head_count), :] for h in range(head_count)], axis=0
    ).astype(jnp.bfloat16)
    contract = (((1,), (1,)), ((), ()))

    width = scores.shape[2]
    chunks = scores.shape[0]
    row_kv = lax.broadcasted_iota(jnp.int32, (rows, width), 0) // (group * pairs)
    col_kv = lax.broadcasted_iota(jnp.int32, (rows, width), 1) % kv_local
    same = row_kv == col_kv

    def score_chunk(c, highest):
        prompt_copy(c, 0).wait()
        s = lax.dot_general(
            q, prompt_keys.at[c].reshape(width, head_dim)[...], contract, preferred_element_type=jnp.float32
        )
        s = jnp.where(same, s, -jnp.inf)
        scores[c] = s
        return jnp.maximum(highest, s.max(-1, keepdims=True))

    prompt_max = lax.fori_loop(
        0, chunks, score_chunk, jnp.full((rows, 1), -jnp.inf, jnp.float32)
    )

    def weigh_chunk(c, carry):
        total, acc = carry
        prompt_copy(c, 1).wait()
        w = jnp.exp2((scores[c] - prompt_max) * factor)
        total = total + w.sum(-1, keepdims=True)
        acc = acc + jnp.dot(
            w.astype(jnp.bfloat16), prompt_values.at[c].reshape(width, head_dim)[...],
            preferred_element_type=jnp.float32,
        )
        return total, acc

    prompt_sum, prompt_acc = lax.fori_loop(
        0, chunks, weigh_chunk,
        (jnp.zeros((rows, 1), jnp.float32), jnp.zeros((rows, head_dim), jnp.float32)),
    )

    forks = fork_ref[...].astype(jnp.float32)
    total_nodes = forks.shape[1]
    ids = lax.broadcasted_iota(jnp.int32, (pairs, total_nodes), 1).astype(jnp.float32)
    pair_at = lax.broadcasted_iota(jnp.int32, (pairs, 1), 0)
    pair_step = pair_at // nodes
    current = (pair_at % nodes + me * nodes).astype(jnp.float32)
    places = [None] * steps
    for step in reversed(range(steps)):
        reached = pair_step >= step
        places[step] = jnp.where(reached, current, -1.0)
        parent = forks[step : step + 1, :]
        parent = jnp.where(parent >= 0.0, parent, ids)
        found = jnp.where(ids == current, parent, 0.0).sum(-1, keepdims=True)
        current = jnp.where(reached, found, current)
    lane = lax.broadcasted_iota(jnp.int32, (pairs, TAIL_WIDTH), 1)
    spot = lane % span // kv_local
    wanted = jnp.broadcast_to(current, (pairs, TAIL_WIDTH))
    for step in range(steps):
        wanted = jnp.where(spot >= pool_tokens + step * nodes, places[step], wanted)
    parity = lane % kv_local
    reachable = wanted >= 0.0

    for copy in pack_copies:
        copy.wait()

    def tail_keys(part, d):
        return packs.at[part, pl.ds(d * join, join)].reshape(TAIL_WIDTH, head_dim)[...]

    def tail_score(d, highest):
        s = lax.dot_general(
            q, tail_keys(0, d), contract, preferred_element_type=jnp.float32
        )
        per_block = BLOCK // span
        blocks = []
        for first in range(0, join, per_block):
            node = owners[d * join + first].astype(jnp.float32)
            for more in range(first + 1, first + per_block):
                node = jnp.maximum(node, owners[d * join + more].astype(jnp.float32))
            blocks.append(node)
        node = jnp.concatenate(blocks, axis=1)[0:1, :]
        seen = reachable & (node == wanted)
        pieces = []
        for k in range(kv_local):
            keep = (seen & (parity == k))[None]
            part = s[k * group * pairs : (k + 1) * group * pairs].reshape(group, pairs, TAIL_WIDTH)
            pieces.append(jnp.where(keep, part, -jnp.inf).reshape(group * pairs, TAIL_WIDTH))
        s = jnp.concatenate(pieces, axis=0)
        tail_scores[d] = s
        return jnp.maximum(highest, s.max(-1, keepdims=True))

    highest = lax.fori_loop(0, dp // join, tail_score, prompt_max)
    carried = jnp.exp2((prompt_max - highest) * factor)

    def tail_weigh(d, carry):
        total, acc = carry
        w = jnp.exp2((tail_scores[d] - highest) * factor)
        total = total + w.sum(-1, keepdims=True)
        acc = acc + jnp.dot(
            w.astype(jnp.bfloat16), tail_keys(1, d),
            preferred_element_type=jnp.float32,
        )
        return total, acc

    denominator, mixed = lax.fori_loop(
        0, dp // join, tail_weigh, (prompt_sum * carried, prompt_acc * carried)
    )
    attended = (mixed / denominator).astype(jnp.bfloat16)
    for h in range(head_count):
        heads[me, :, h * head_dim : (h + 1) * head_dim] = attended[h * pairs : (h + 1) * pairs]

    head_copies = []
    for hop in range(1, dp):
        copy = pltpu.make_async_remote_copy(
            src_ref=heads.at[me],
            dst_ref=heads.at[me],
            send_sem=head_send.at[hop],
            recv_sem=head_recv.at[hop],
            device_id={"dp": lax.rem(me + hop, dp)},
            device_id_type=MESH,
        )
        copy.start()
        head_copies.append(copy)
    weight_copy.wait()
    for copy in head_copies:
        copy.wait()

    columns = weight.shape[1]
    per_tensor = dp // tensor
    gathered = heads[...].reshape(dp * pairs, head_count * head_dim)
    part_copies = []
    for at in range(columns // tile):
        here = slice(at * tile, (at + 1) * tile)
        product = jnp.dot(gathered, weight[:, here], preferred_element_type=jnp.float32)
        partial[at] = product.astype(jnp.bfloat16).reshape(tensor, per_tensor * pairs, tile)
        for hop in range(1, tensor):
            peer = lax.rem(me_tensor + hop, tensor)
            copy = pltpu.make_async_remote_copy(
                src_ref=partial.at[at, peer],
                dst_ref=landed.at[at, hop],
                send_sem=part_send.at[at, hop],
                recv_sem=part_recv.at[at, hop],
                device_id={"tensor": peer},
                device_id_type=MESH,
            )
            copy.start()
            part_copies.append(copy)
    for at in range(columns // tile):
        here = slice(at * tile, (at + 1) * tile)
        for copy in part_copies[at * (tensor - 1) : (at + 1) * (tensor - 1)]:
            copy.wait()
        total = partial[at, me_tensor].astype(jnp.float32)
        for hop in range(1, tensor):
            total = total + landed[at, hop].astype(jnp.float32)
        for s in range(steps):
            for block in range(per_tensor):
                own = slice(block * nodes, (block + 1) * nodes)
                at_row = block * pairs + s * nodes
                out_ref[s, own, here] = (
                    residual_ref[s, own, here].astype(jnp.float32)
                    + total[at_row : at_row + nodes]
                ).astype(jnp.bfloat16)


def local(
    dp, tensor,
    query, new_kv, tail_pool, page_table, tail_len, fork_parent, prompt_kv, out_weight, residual,
):
    steps, nodes, head_count, head_dim = query.shape
    pages, page, kv_local, _ = tail_pool.shape
    prompt = prompt_kv.shape[0]
    columns = out_weight.shape[1]
    pairs = steps * nodes
    rows = pairs * head_count
    per_tensor = dp // tensor
    span = (nodes * page + pairs) * kv_local
    tile = min(512, columns)
    width = 1024
    chunks = prompt * kv_local // width
    bf16 = jnp.bfloat16

    dims = (dp, tensor, steps, nodes, head_count, kv_local, head_dim, pages, page, tile)
    vmem = pl.BlockSpec(memory_space=pltpu.VMEM)
    tiles = columns // tile
    dma = pltpu.SemaphoreType.DMA
    return pl.pallas_call(
        functools.partial(kernel, dims),
        out_shape=pltpu.VMEM(residual.shape, bf16),
        in_specs=[pl.BlockSpec(memory_space=pltpu.HBM)] * 9,
        out_specs=vmem,
        scratch_shapes=[
            pltpu.SMEM(page_table.shape[::-1], jnp.int32),
            pltpu.SMEM(tail_len.shape, jnp.int32),
            pltpu.VMEM((rows, head_dim), bf16),
            pltpu.VMEM(fork_parent.shape, jnp.int32),
            pltpu.VMEM(residual.shape, bf16),
            pltpu.VMEM(tail_pool.shape, bf16),
            pltpu.VMEM((rows, head_dim), jnp.float32),
            pltpu.VMEM((chunks, width // kv_local, kv_local, head_dim), bf16),
            pltpu.VMEM((chunks, width // kv_local, kv_local, head_dim), bf16),
            pltpu.VMEM((chunks, rows, width), jnp.float32),
            pltpu.VMEM((dp * span // TAIL_WIDTH, rows, TAIL_WIDTH), jnp.float32),
            pltpu.VMEM((2, dp, span // kv_local, kv_local, head_dim), bf16),
            pltpu.VMEM((dp, 16, BLOCK), bf16),
            pltpu.VMEM(out_weight.shape, bf16),
            pltpu.VMEM((dp, pairs, head_count * head_dim), bf16),
            pltpu.VMEM((tiles, tensor, per_tensor * pairs, tile), bf16),
            pltpu.VMEM((tiles, tensor, per_tensor * pairs, tile), bf16),
            dma((6,)),
            dma,
            dma((2,)),
            dma((2, chunks)),
            dma((2, dp)),
            dma((2, dp)),
            dma((dp,)),
            dma((dp,)),
            dma((dp,)),
            dma((dp,)),
            dma((tiles, tensor)),
            dma((tiles, tensor)),
        ],
        compiler_params=pltpu.CompilerParams(
            collective_id=0, has_side_effects=True, vmem_limit_bytes=63 * 1024 * 1024
        ),
    )(
        page_table.T,
        tail_len,
        query.reshape(rows, head_dim),
        fork_parent,
        residual,
        tail_pool,
        prompt_kv,
        new_kv.reshape(pairs, kv_local, 2 * head_dim),
        out_weight,
    )


def solution(mesh):
    in_specs = (
        P(None, ("groups", "dp"), "tensor", None),
        P(None, ("groups", "dp"), "tensor", None),
        P(("groups", "dp"), None, "tensor", None),
        P(("groups", "dp"), None),
        P(("groups", "dp")),
        P(None, "groups"),
        P("groups", "tensor", None),
        P("tensor", "dp"),
        P(None, ("groups", "tensor"), "dp"),
    )
    out_specs = P(None, ("groups", "tensor"), "dp")
    body = functools.partial(local, mesh.shape["dp"], mesh.shape["tensor"])
    return jax.shard_map(body, mesh=mesh, in_specs=in_specs, out_specs=out_specs, check_vma=False)
```

```python
import functools
import math

import jax
import jax.numpy as jnp
from jax import lax
from jax.experimental import pallas as pl
from jax.experimental.pallas import tpu as pltpu
from jax.sharding import PartitionSpec as P

MESH = pl.DeviceIdType.MESH
BLOCK = 128
TAIL_WIDTH = 256


def kernel(
    dims, table_in, len_in, q_in, fork_in, residual_in, pool_in, prompt_ref, new_ref,
    weight_ref, out_ref,
    table_ref, len_ref, q_ref, fork_ref, residual_ref, pool_ref,
    q_flat, prompt_keys, prompt_values, scores, tail_scores, packs, owners, weight, heads,
    partial, landed,
    in_sem, weight_sem, own_sem, prompt_sem, pack_send, pack_recv, owner_send, owner_recv,
    head_send, head_recv, part_send, part_recv,
):
    dp, tensor, steps, nodes, head_count, kv_local, head_dim, pages, page, tile = dims
    pairs = steps * nodes
    rows = pairs * head_count
    group = head_count // kv_local
    pool_rows = pages * page * kv_local
    new_rows = pairs * kv_local
    me = lax.axis_index("dp")
    me_tensor = lax.axis_index("tensor")
    factor = head_dim ** (-0.5) * math.log2(math.e)

    total_chunks, chunk_prompt = prompt_keys.shape[0], prompt_keys.shape[1]
    pool_tokens = nodes * page
    span = (pool_tokens + pairs) * kv_local
    join = TAIL_WIDTH // span

    small_copies = [
        pltpu.make_async_copy(source, target, in_sem.at[at])
        for at, (source, target) in enumerate(
            (
                (table_in, table_ref), (len_in, len_ref), (pool_in, pool_ref), (q_in, q_ref),
                (fork_in, fork_ref), (residual_in, residual_ref),
            )
        )
    ]
    for copy in small_copies[:3]:
        copy.start()
    own_copies = []
    for part in range(2):
        lanes = slice(part * head_dim, (part + 1) * head_dim)
        own_copies.append(
            pltpu.make_async_copy(
                new_ref.at[:, :, lanes], packs.at[part, me, pool_tokens : pool_tokens + pairs],
                own_sem.at[part],
            )
        )
    for copy in own_copies + small_copies[3:]:
        copy.start()

    def prompt_copy(c, part):
        return pltpu.make_async_copy(
            prompt_ref.at[
                pl.ds(c * chunk_prompt, chunk_prompt), :,
                part * head_dim : (part + 1) * head_dim,
            ],
            (prompt_values if part else prompt_keys).at[c],
            prompt_sem.at[part, c],
        )

    for part in range(2):
        for c in range(total_chunks):
            prompt_copy(c, part).start()
    weight_copy = pltpu.make_async_copy(weight_ref, weight, weight_sem)
    weight_copy.start()

    barrier = pltpu.get_barrier_semaphore()
    for hop in range(1, dp):
        pl.semaphore_signal(
            barrier, inc=1, device_id={"dp": lax.rem(me + hop, dp)}, device_id_type=MESH
        )
    for hop in range(1, tensor):
        pl.semaphore_signal(
            barrier, inc=1, device_id={"tensor": lax.rem(me_tensor + hop, tensor)},
            device_id_type=MESH,
        )

    for copy in small_copies[:3]:
        copy.wait()
    lane = lax.broadcasted_iota(jnp.int32, (16, BLOCK), 1)
    spot = lane % span // kv_local
    owner = (spot - pool_tokens) % nodes
    for n in range(nodes):
        owner = jnp.where(
            spot // page == n, jnp.where(spot % page < len_ref[n], n, -1 - me * nodes), owner
        )
        for part in range(2):
            lanes = slice(part * head_dim, (part + 1) * head_dim)
            packs[part, me, n * page : (n + 1) * page] = pool_ref[table_ref[0, n], :, :, lanes]
    owner = jnp.where(lane // span == me % (BLOCK // span), owner + me * nodes, -1)
    owners[me] = owner.astype(jnp.float32).astype(jnp.bfloat16)
    for copy in own_copies:
        copy.wait()
    pl.semaphore_wait(barrier, dp + tensor - 2)

    pack_copies = []
    for hop in range(1, dp):
        for buffer, send, recv in (
            (owners.at[me], owner_send.at[hop], owner_recv.at[hop]),
            (packs.at[0, me], pack_send.at[0, hop], pack_recv.at[0, hop]),
            (packs.at[1, me], pack_send.at[1, hop], pack_recv.at[1, hop]),
        ):
            copy = pltpu.make_async_remote_copy(
                src_ref=buffer,
                dst_ref=buffer,
                send_sem=send,
                recv_sem=recv,
                device_id={"dp": lax.rem(me + hop, dp)},
                device_id_type=MESH,
            )
            copy.start()
            pack_copies.append(copy)

    for copy in small_copies[3:]:
        copy.wait()
    q_flat[...] = q_ref[...].astype(jnp.float32)
    q = jnp.concatenate(
        [q_flat[pl.ds(h, pairs, stride=head_count), :] for h in range(head_count)], axis=0
    ).astype(jnp.bfloat16)
    contract = (((1,), (1,)), ((), ()))

    width = scores.shape[2]
    chunks = scores.shape[0]
    row_kv = lax.broadcasted_iota(jnp.int32, (rows, width), 0) // (group * pairs)
    col_kv = lax.broadcasted_iota(jnp.int32, (rows, width), 1) % kv_local
    same = row_kv == col_kv

    def score_chunk(c, highest):
        prompt_copy(c, 0).wait()
        s = lax.dot_general(
            q, prompt_keys.at[c].reshape(width, head_dim)[...], contract, preferred_element_type=jnp.float32
        )
        s = jnp.where(same, s, -jnp.inf)
        scores[c] = s
        return jnp.maximum(highest, s.max(-1, keepdims=True))

    prompt_max = lax.fori_loop(
        0, chunks, score_chunk, jnp.full((rows, 1), -jnp.inf, jnp.float32)
    )

    def weigh_chunk(c, carry):
        total, acc = carry
        prompt_copy(c, 1).wait()
        w = jnp.exp2((scores[c] - prompt_max) * factor)
        total = total + w.sum(-1, keepdims=True)
        acc = acc + jnp.dot(
            w.astype(jnp.bfloat16), prompt_values.at[c].reshape(width, head_dim)[...],
            preferred_element_type=jnp.float32,
        )
        return total, acc

    prompt_sum, prompt_acc = lax.fori_loop(
        0, chunks, weigh_chunk,
        (jnp.zeros((rows, 1), jnp.float32), jnp.zeros((rows, head_dim), jnp.float32)),
    )

    forks = fork_ref[...].astype(jnp.float32)
    total_nodes = forks.shape[1]
    ids = lax.broadcasted_iota(jnp.int32, (pairs, total_nodes), 1).astype(jnp.float32)
    pair_at = lax.broadcasted_iota(jnp.int32, (pairs, 1), 0)
    pair_step = pair_at // nodes
    current = (pair_at % nodes + me * nodes).astype(jnp.float32)
    places = [None] * steps
    for step in reversed(range(steps)):
        reached = pair_step >= step
        places[step] = jnp.where(reached, current, -1.0)
        parent = forks[step : step + 1, :]
        parent = jnp.where(parent >= 0.0, parent, ids)
        found = jnp.where(ids == current, parent, 0.0).sum(-1, keepdims=True)
        current = jnp.where(reached, found, current)
    lane = lax.broadcasted_iota(jnp.int32, (pairs, TAIL_WIDTH), 1)
    spot = lane % span // kv_local
    wanted = jnp.broadcast_to(current, (pairs, TAIL_WIDTH))
    for step in range(steps):
        wanted = jnp.where(spot >= pool_tokens + step * nodes, places[step], wanted)
    parity = lane % kv_local
    reachable = wanted >= 0.0

    for copy in pack_copies:
        copy.wait()

    def tail_keys(part, d):
        return packs.at[part, pl.ds(d * join, join)].reshape(TAIL_WIDTH, head_dim)[...]

    def tail_score(d, highest):
        s = lax.dot_general(
            q, tail_keys(0, d), contract, preferred_element_type=jnp.float32
        )
        per_block = BLOCK // span
        blocks = []
        for first in range(0, join, per_block):
            node = owners[d * join + first].astype(jnp.float32)
            for more in range(first + 1, first + per_block):
                node = jnp.maximum(node, owners[d * join + more].astype(jnp.float32))
            blocks.append(node)
        node = jnp.concatenate(blocks, axis=1)[0:1, :]
        seen = reachable & (node == wanted)
        pieces = []
        for k in range(kv_local):
            keep = (seen & (parity == k))[None]
            part = s[k * group * pairs : (k + 1) * group * pairs].reshape(group, pairs, TAIL_WIDTH)
            pieces.append(jnp.where(keep, part, -jnp.inf).reshape(group * pairs, TAIL_WIDTH))
        s = jnp.concatenate(pieces, axis=0)
        tail_scores[d] = s
        return jnp.maximum(highest, s.max(-1, keepdims=True))

    highest = lax.fori_loop(0, dp // join, tail_score, prompt_max)
    carried = jnp.exp2((prompt_max - highest) * factor)

    def tail_weigh(d, carry):
        total, acc = carry
        w = jnp.exp2((tail_scores[d] - highest) * factor)
        total = total + w.sum(-1, keepdims=True)
        acc = acc + jnp.dot(
            w.astype(jnp.bfloat16), tail_keys(1, d),
            preferred_element_type=jnp.float32,
        )
        return total, acc

    denominator, mixed = lax.fori_loop(
        0, dp // join, tail_weigh, (prompt_sum * carried, prompt_acc * carried)
    )
    attended = (mixed / denominator).astype(jnp.bfloat16)
    for h in range(head_count):
        heads[me, :, h * head_dim : (h + 1) * head_dim] = attended[h * pairs : (h + 1) * pairs]

    def partner(index, hop):
        bit = 1
        while bit <= hop:
            if hop & bit:
                index = index + bit - 2 * bit * (index // bit % 2)
            bit *= 2
        return index

    head_copies = []
    for hop in range(1, dp):
        copy = pltpu.make_async_remote_copy(
            src_ref=heads.at[me],
            dst_ref=heads.at[me],
            send_sem=head_send.at[hop],
            recv_sem=head_recv.at[hop],
            device_id={"dp": partner(me, hop)},
            device_id_type=MESH,
        )
        copy.start()
        head_copies.append(copy)
    weight_copy.wait()

    columns = weight.shape[1]
    per_tensor = dp // tensor

    def part_copy(at, hop):
        peer = lax.rem(me_tensor + hop, tensor)
        return pltpu.make_async_remote_copy(
            src_ref=partial.at[peer, at],
            dst_ref=landed.at[hop, at],
            send_sem=part_send.at[hop, at],
            recv_sem=part_recv.at[hop, at],
            device_id={"tensor": peer},
            device_id_type=MESH,
        )

    for turn in range(0, tensor, 2):
        block = partner(me // per_tensor, turn) // 2 * 2
        for hop in range(max(1, turn * per_tensor), (turn + 2) * per_tensor):
            head_copies[hop - 1].wait_recv()
        gathered = heads[pl.ds(block * per_tensor, 2 * per_tensor)].reshape(
            2 * per_tensor * pairs, head_count * head_dim
        )
        for at in range(columns // tile):
            here = slice(at * tile, (at + 1) * tile)
            product = jnp.dot(gathered, weight[:, here], preferred_element_type=jnp.float32)
            product = product.astype(jnp.bfloat16)
            partial[block, at] = product[: per_tensor * pairs]
            partial[block + 1, at] = product[per_tensor * pairs :]
            for hop in range(1, tensor):

                @pl.when(lax.rem(me_tensor + hop, tensor) // 2 == block // 2)
                def _():
                    part_copy(at, hop).start()

    for copy in head_copies:
        copy.wait_send()
    for at in range(columns // tile):
        here = slice(at * tile, (at + 1) * tile)
        for hop in range(1, tensor):
            part_copy(at, hop).wait()
        total = partial[me_tensor, at].astype(jnp.float32)
        for hop in range(1, tensor):
            total = total + landed[hop, at].astype(jnp.float32)
        for s in range(steps):
            for block in range(per_tensor):
                own = slice(block * nodes, (block + 1) * nodes)
                at_row = block * pairs + s * nodes
                out_ref[s, own, here] = (
                    residual_ref[s, own, here].astype(jnp.float32)
                    + total[at_row : at_row + nodes]
                ).astype(jnp.bfloat16)


def local(
    dp, tensor,
    query, new_kv, tail_pool, page_table, tail_len, fork_parent, prompt_kv, out_weight, residual,
):
    steps, nodes, head_count, head_dim = query.shape
    pages, page, kv_local, _ = tail_pool.shape
    prompt = prompt_kv.shape[0]
    columns = out_weight.shape[1]
    pairs = steps * nodes
    rows = pairs * head_count
    per_tensor = dp // tensor
    span = (nodes * page + pairs) * kv_local
    tile = min(512, columns)
    width = 1024
    chunks = prompt * kv_local // width
    bf16 = jnp.bfloat16

    dims = (dp, tensor, steps, nodes, head_count, kv_local, head_dim, pages, page, tile)
    vmem = pl.BlockSpec(memory_space=pltpu.VMEM)
    tiles = columns // tile
    dma = pltpu.SemaphoreType.DMA
    return pl.pallas_call(
        functools.partial(kernel, dims),
        out_shape=pltpu.VMEM(residual.shape, bf16),
        in_specs=[pl.BlockSpec(memory_space=pltpu.HBM)] * 9,
        out_specs=vmem,
        scratch_shapes=[
            pltpu.SMEM(page_table.shape[::-1], jnp.int32),
            pltpu.SMEM(tail_len.shape, jnp.int32),
            pltpu.VMEM((rows, head_dim), bf16),
            pltpu.VMEM(fork_parent.shape, jnp.int32),
            pltpu.VMEM(residual.shape, bf16),
            pltpu.VMEM(tail_pool.shape, bf16),
            pltpu.VMEM((rows, head_dim), jnp.float32),
            pltpu.VMEM((chunks, width // kv_local, kv_local, head_dim), bf16),
            pltpu.VMEM((chunks, width // kv_local, kv_local, head_dim), bf16),
            pltpu.VMEM((chunks, rows, width), jnp.float32),
            pltpu.VMEM((dp * span // TAIL_WIDTH, rows, TAIL_WIDTH), jnp.float32),
            pltpu.VMEM((2, dp, span // kv_local, kv_local, head_dim), bf16),
            pltpu.VMEM((dp, 16, BLOCK), bf16),
            pltpu.VMEM(out_weight.shape, bf16),
            pltpu.VMEM((dp, pairs, head_count * head_dim), bf16),
            pltpu.VMEM((tensor, tiles, per_tensor * pairs, tile), bf16),
            pltpu.VMEM((tensor, tiles, per_tensor * pairs, tile), bf16),
            dma((6,)),
            dma,
            dma((2,)),
            dma((2, chunks)),
            dma((2, dp)),
            dma((2, dp)),
            dma((dp,)),
            dma((dp,)),
            dma((dp,)),
            dma((dp,)),
            dma((tensor, tiles)),
            dma((tensor, tiles)),
        ],
        compiler_params=pltpu.CompilerParams(
            collective_id=0, has_side_effects=True, vmem_limit_bytes=63 * 1024 * 1024
        ),
    )(
        page_table.T,
        tail_len,
        query.reshape(rows, head_dim),
        fork_parent,
        residual,
        tail_pool,
        prompt_kv,
        new_kv.reshape(pairs, kv_local, 2 * head_dim),
        out_weight,
    )


def solution(mesh):
    in_specs = (
        P(None, ("groups", "dp"), "tensor", None),
        P(None, ("groups", "dp"), "tensor", None),
        P(("groups", "dp"), None, "tensor", None),
        P(("groups", "dp"), None),
        P(("groups", "dp")),
        P(None, "groups"),
        P("groups", "tensor", None),
        P("tensor", "dp"),
        P(None, ("groups", "tensor"), "dp"),
    )
    out_specs = P(None, ("groups", "tensor"), "dp")
    body = functools.partial(local, mesh.shape["dp"], mesh.shape["tensor"])
    return jax.shard_map(body, mesh=mesh, in_specs=in_specs, out_specs=out_specs, check_vma=False)
```
